32 devices in a mesh: ens: 2 (over x), tile: 8 (over z, y), comp: 2 (over core).
Axes of the slice: x: 2, y: 2, z: 4, core: 2. Of those that a mesh axis runs over, the one named last changes fastest.
Arguments:
- increment: bfloat16 [64, 128, 256], P(('ens', 'tile'), None, 'comp'), parts along dimension 0, may hold values from -6 to 6
- land_sea: int32 [32, 128], P('tile'), may hold values 0 or 1
- kernel_x: float32 [41, 256], P(None, 'comp'), may hold values from -1 to 1
- kernel_y: float32 [41, 256], P(None, 'comp'), may hold values from -1 to 1
- balance: bfloat16 [8, 256, 256], P('tile', 'comp'), may hold values from -0.375 to 0.375
Outputs:
- filtered: bfloat16 [64, 128, 256], P('ens', 'tile', 'comp'), parts along dimension 0
The draws below stay inside these ranges and needn't reach their ends.
There are 2 independent parts, one for each index of `ens`. The reference program is written for one: setup_inputs(seed, part) draws one part's arguments, and reference() takes and returns one part's arrays. A program takes and returns all parts, laid end to end along the dimension named above; an argument that names none is the same for every part. Nothing has to cross between parts.
All inputs are finite; a program needn't handle non-finite values. No bound on the sum of `land_sea` on one device may be relied on, other than what follows from the above.
Results may differ from the reference program's by a relative error of at most 0.0057.
Values may be sent and summed in bfloat16 or wider, within the bound.
A program may use at most 64 MiB of HBM per device.

```python
import jax
import jax.numpy as jnp
from jax import lax

C = 256
TAPS = 41
RY = 4
NY = 32
NX = 128
NS = 8


def place_ends(array, key, low, largest):
    extent = array.shape
    spot = [jax.random.randint(jax.random.fold_in(key, axis), (), 0, extent[axis]) for axis in range(len(extent))]
    array = array.at[tuple(spot)].set(low)
    longest = extent.index(max(extent))
    spot[longest] = (spot[longest] + 1) % extent[longest]
    return array.at[tuple(spot)].set(largest)


def block_levels(rng, extent, split, low, largest):
    factor_of = 1.0
    for position, blocks in split:
        heights = jax.random.uniform(jax.random.fold_in(jax.random.fold_in(rng, 6), position), (blocks,), jnp.float32, low / len(split), largest / len(split))
        factor_of = factor_of * jnp.repeat(jnp.exp(heights), extent[position] // blocks).reshape((-1,) + (1,) * (len(extent) - 1 - position))
    return factor_of


def gaussian(stream_key, extent, width, reach, pieces=(), kind=jnp.bfloat16):
    gain = block_levels(stream_key, extent, pieces, -0.22, 0.18) if pieces else 1.0
    drawn = jax.random.normal(stream_key, extent, jnp.float32) * width * gain
    return jnp.minimum(jnp.maximum(drawn, -reach), reach).astype(kind)


def setup_inputs(seed: int = 0, part: int = 0) -> dict:
    arg_keys = jax.random.split(jax.random.key(seed), 6)
    part_splits = jax.random.split(jax.random.fold_in(arg_keys[5], part), 6)
    increment = gaussian(part_splits[0], (NY, NX, C), 1.0, 6.0, ((0, 8), (2, 2)))
    land_sea = place_ends((jax.random.randint(arg_keys[1], (NY, NX), 0, 10) < 7).astype(jnp.int32), jax.random.fold_in(arg_keys[1], 1), 0, 1)
    kernel_x = gaussian(arg_keys[2], (TAPS, C), TAPS ** -0.5, 1.0, ((1, 2),), jnp.float32)
    kernel_y = gaussian(arg_keys[3], (TAPS, C), TAPS ** -0.5, 1.0, ((1, 2),), jnp.float32)
    balance = gaussian(arg_keys[4], (NS, C, C), C ** -0.5, 0.375, ((0, 8), (1, 2)))
    return {"increment": increment, "land_sea": land_sea, "kernel_x": kernel_x, "kernel_y": kernel_y, "balance": balance}


def reference(increment, land_sea, kernel_x, kernel_y, balance):
    sea = land_sea.astype(jnp.float32)[:, :, None]
    masked = increment.astype(jnp.float32) * sea
    half_taps = (TAPS - 1) // 2
    zonal = jnp.zeros(masked.shape, jnp.float32)
    for offset in range(TAPS):
        zonal = zonal + kernel_x[offset].astype(jnp.float32) * jnp.roll(masked, half_taps - offset, axis=1)
    zonal = (zonal * sea).astype(jnp.bfloat16)
    rows_all = zonal.shape[0]
    banded = zonal.reshape((NS, RY) + zonal.shape[1:])

    def apply_block(pair):
        return jnp.einsum("rxj,ij->rxi", pair[0].astype(jnp.float32), pair[1].astype(jnp.float32)).astype(jnp.bfloat16)

    mixed = lax.map(apply_block, (banded, balance)).reshape(zonal.shape)
    padded = jnp.pad(mixed.astype(jnp.float32), ((half_taps, half_taps), (0, 0), (0, 0)))
    filtered = jnp.zeros(mixed.shape, jnp.float32)
    for offset in range(TAPS):
        filtered = filtered + kernel_y[offset].astype(jnp.float32) * padded[offset:offset + rows_all]
    return filtered.astype(jnp.bfloat16)
```

```python
import functools

import jax
import jax.numpy as jnp
from jax import lax
from jax.experimental import pallas as pl
from jax.experimental.pallas import tpu as pltpu
from jax.sharding import PartitionSpec as P

MESH = pl.DeviceIdType.MESH
F32 = jnp.float32
BF16 = jnp.bfloat16


def kernel(
    tiles, reach,
    inc_hbm, sea_hbm, kx_hbm, ky_hbm, bal_hbm, out_ref,
    inc, sea, kx, ky, bal, sea8, mask, nat, ext, zbuf, msend, mrecv, taps_y, acc,
    in_sem, zsend_sem, zrecv_sem, msend_sem, mrecv_sem,
):
    me = lax.axis_index("tile")
    core = lax.axis_index("comp")
    rows, columns, lanes = inc.shape
    half_x = columns // 2
    half = tiles // 2
    width = columns // tiles
    taps = kx.shape[0]
    reach_y = (taps - 1) // 2

    loads = [
        pltpu.make_async_copy(src, dst, in_sem.at[n])
        for n, (src, dst) in enumerate(
            ((sea_hbm, sea), (inc_hbm, inc), (kx_hbm, kx), (bal_hbm, bal), (ky_hbm, ky))
        )
    ]
    for load in loads:
        load.start()

    barrier = pltpu.get_barrier_semaphore()

    @pl.loop(1, tiles)
    def _(d):
        pl.semaphore_signal(
            barrier, inc=1, device_id={"tile": lax.rem(me + d, tiles)}, device_id_type=MESH
        )

    pl.semaphore_signal(barrier, inc=1, device_id={"comp": 1 - core}, device_id_type=MESH)

    loads[0].wait()
    sea8[...] = jnp.zeros_like(sea8)
    sea8[0:rows] = sea[...].astype(F32)
    row_of = lax.broadcasted_iota(jnp.int32, (8, lanes), 0)
    for r in range(rows):
        spread = lax.dot_general(
            sea8[...], (row_of == r).astype(F32), (((0,), (0,)), ((), ())),
            preferred_element_type=F32,
        )
        for h in range(2):
            mask[h * rows + r] = spread[h * half_x : (h + 1) * half_x]

    loads[1].wait()
    for r in range(rows):
        for h in range(2):
            j = h * rows + r
            nat[j] = inc[r, h * half_x : (h + 1) * half_x, :].astype(F32) * mask[j]
    for b in range(half_x // 8):
        ext[reach + 8 * b : reach + 8 * b + 8] = jnp.swapaxes(nat[:, 8 * b : 8 * b + 8, :], 0, 1)
    for i in range(reach):
        ext[i] = pltpu.roll(ext[i + half_x], rows, axis=0)
        ext[reach + half_x + i] = pltpu.roll(ext[reach + i], rows, axis=0)

    def chunk_of(step):
        return lax.rem(me + 1 + step, half)

    def exchange(q):
        return pltpu.make_async_remote_copy(
            src_ref=zbuf.at[q, core],
            dst_ref=zbuf.at[q, core],
            send_sem=zsend_sem.at[q],
            recv_sem=zrecv_sem.at[q],
            device_id={"comp": 1 - core},
            device_id_type=MESH,
        )

    def deliver(q, h):
        p = h * half + q
        return pltpu.make_async_remote_copy(
            src_ref=msend.at[q, h],
            dst_ref=mrecv.at[me],
            send_sem=msend_sem.at[p],
            recv_sem=mrecv_sem.at[me],
            device_id={"tile": p},
            device_id_type=MESH,
        )

    def zonal(q):
        base = pl.multiple_of(q * width, width)
        total = jnp.zeros((width, 8, lanes), F32)
        for k in range(taps):
            total = total + kx[k : k + 1, :][None] * ext[pl.ds(base + k, width)]
        cells = jnp.swapaxes(total, 0, 1) * mask[:, pl.ds(base, width), :]
        zbuf[q, core] = cells.astype(BF16)

    def finish(q):
        exchange(q).wait_recv()
        lhs = jnp.concatenate(
            [zbuf[q, c].reshape(8 * width, lanes) for c in range(2)], axis=-1
        )
        mixed = lax.dot_general(
            lhs, bal[0], (((1,), (1,)), ((), ())), preferred_element_type=F32
        )
        msend[q] = mixed.astype(BF16).reshape(2, rows, width, lanes)
        for h in range(2):
            p = h * half + q

            @pl.when(p == me)
            def _():
                mrecv[me] = msend[q, h]

            @pl.when(p != me)
            def _():
                deliver(q, h).start()

    loads[2].wait()
    zonal(chunk_of(0))
    pl.semaphore_wait(barrier, tiles)
    exchange(chunk_of(0)).start()
    loads[3].wait()

    @pl.loop(1, half)
    def _(step):
        q = chunk_of(step)
        zonal(q)
        exchange(q).start()
        finish(chunk_of(step - 1))

    finish(chunk_of(half - 1))

    loads[4].wait()
    acc[...] = jnp.zeros_like(acc)
    window = min(tiles, 2 * -(-reach_y // rows) + 1)
    near = window // 2 if window < tiles else 0
    margin = (taps_y.shape[0] - taps) // 2
    taps_y[...] = jnp.zeros_like(taps_y)
    for k in range(taps):
        taps_y[margin + k] = jnp.broadcast_to(ky[k : k + 1, :], (8, lanes))

    def gather(s):
        @pl.when(s != me)
        def _():
            pltpu.make_async_remote_copy(
                src_ref=mrecv.at[s],
                dst_ref=mrecv.at[s],
                send_sem=msend_sem.at[s],
                recv_sem=mrecv_sem.at[s],
                device_id={"tile": s},
                device_id_type=MESH,
            ).wait_recv()

        band = mrecv[s].astype(F32).reshape(rows, width // 8, 8, lanes)
        first = jnp.minimum(jnp.maximum(s - near, 0), tiles - window)
        for d in range(window):
            b = first + d
            start = rows * (s - b) + reach_y + margin
            for o in range(rows):
                y = rows * b + o
                total = acc[y]
                for i in range(rows):
                    total = total + taps_y[start + i - o][None] * band[i]
                acc[y] = total

    @pl.loop(0, half)
    def _(step):
        s = lax.rem(me + half - 1 - step + tiles, half)
        for h in range(2):
            gather(h * half + s)

    @pl.loop(0, tiles)
    def _(b):
        part = acc[pl.ds(rows * b, rows)]
        out_ref[pl.ds(rows * b, rows)] = part.reshape(rows, width, lanes).astype(BF16)

    @pl.loop(0, half)
    def _(q):
        exchange(q).wait_send()
        for h in range(2):
            @pl.when(h * half + q != me)
            def _():
                deliver(q, h).wait_send()


def per_device(tiles, increment, land_sea, kernel_x, kernel_y, balance):
    rows, columns, lanes = increment.shape
    taps = kernel_x.shape[0]
    reach = (taps - 1) // 2
    half_x, half, width = columns // 2, tiles // 2, columns // tiles
    ny = rows * tiles
    window = min(tiles, 2 * -(-reach // rows) + 1)
    margin = max(rows * (window - 1) + rows - 1 - reach, 0)
    vmem = pltpu.VMEM
    return pl.pallas_call(
        functools.partial(kernel, tiles, reach),
        out_shape=jax.ShapeDtypeStruct((ny, width, lanes), BF16),
        in_specs=[pl.BlockSpec(memory_space=pl.ANY)] * 5,
        out_specs=pl.BlockSpec(memory_space=pltpu.VMEM),
        scratch_shapes=[
            vmem(increment.shape, BF16),
            vmem(land_sea.shape, jnp.int32),
            vmem(kernel_x.shape, F32),
            vmem(kernel_y.shape, F32),
            vmem(balance.shape, BF16),
            vmem((8, columns), F32),
            vmem((2 * rows, half_x, lanes), F32),
            vmem((2 * rows, half_x, lanes), F32),
            vmem((half_x + 2 * reach, 8, lanes), F32),
            vmem((half, 2, 2 * rows, width, lanes), BF16),
            vmem((half, 2, rows, width, lanes), BF16),
            vmem((tiles, rows, width, lanes), BF16),
            vmem((taps + 2 * margin, 8, lanes), F32),
            vmem((ny, width // 8, 8, lanes), F32),
            pltpu.SemaphoreType.DMA((5,)),
            pltpu.SemaphoreType.DMA((half,)),
            pltpu.SemaphoreType.DMA((half,)),
            pltpu.SemaphoreType.DMA((tiles,)),
            pltpu.SemaphoreType.DMA((tiles,)),
        ],
        compiler_params=pltpu.CompilerParams(
            collective_id=0, has_side_effects=True, vmem_limit_bytes=48 * 1024 * 1024
        ),
    )(increment, land_sea, kernel_x, kernel_y, balance)


def solution(mesh):
    return jax.shard_map(
        functools.partial(per_device, mesh.shape["tile"]),
        mesh=mesh,
        in_specs=(
            P(("ens", "tile"), None, "comp"),
            P("tile", None),
            P(None, "comp"),
            P(None, "comp"),
            P("tile", "comp", None),
        ),
        out_specs=P("ens", "tile", "comp"),
        check_vma=False,
    )
```

```python
import functools

import jax
import jax.numpy as jnp
from jax import lax
from jax.experimental import pallas as pl
from jax.experimental.pallas import tpu as pltpu
from jax.sharding import PartitionSpec as P

MESH = pl.DeviceIdType.MESH
F32 = jnp.float32
BF16 = jnp.bfloat16


def kernel(
    tiles, reach,
    inc_hbm, sea_hbm, kx_hbm, ky_hbm, bal_hbm, out_ref,
    inc, sea, kx, ky, bal, sea8, mask, nat, ext, zbuf, msend, mrecv, taps_y, acc,
    in_sem, zsend_sem, zrecv_sem, msend_sem, mrecv_sem,
):
    me = lax.axis_index("tile")
    core = lax.axis_index("comp")
    rows, columns, lanes = inc.shape
    half_x = columns // 2
    half = tiles // 2
    width = columns // tiles
    taps = kx.shape[0]
    reach_y = (taps - 1) // 2

    loads = [
        pltpu.make_async_copy(src, dst, in_sem.at[n])
        for n, (src, dst) in enumerate(
            ((sea_hbm, sea), (inc_hbm, inc), (kx_hbm, kx), (bal_hbm, bal), (ky_hbm, ky))
        )
    ]
    for load in loads:
        load.start()

    barrier = pltpu.get_barrier_semaphore()

    @pl.loop(1, tiles)
    def _(d):
        pl.semaphore_signal(
            barrier, inc=1, device_id={"tile": lax.rem(me + d, tiles)}, device_id_type=MESH
        )

    pl.semaphore_signal(barrier, inc=1, device_id={"comp": 1 - core}, device_id_type=MESH)

    loads[0].wait()
    sea8[...] = jnp.zeros_like(sea8)
    sea8[0:rows] = sea[...].astype(F32)
    row_of = lax.broadcasted_iota(jnp.int32, (8, lanes), 0)
    for r in range(rows):
        spread = lax.dot_general(
            sea8[...], (row_of == r).astype(F32), (((0,), (0,)), ((), ())),
            preferred_element_type=F32,
        )
        for h in range(2):
            mask[h * rows + r] = spread[h * half_x : (h + 1) * half_x]

    loads[1].wait()
    for r in range(rows):
        for h in range(2):
            j = h * rows + r
            nat[j] = inc[r, h * half_x : (h + 1) * half_x, :].astype(F32) * mask[j]
    for b in range(half_x // 8):
        ext[reach + 8 * b : reach + 8 * b + 8] = jnp.swapaxes(nat[:, 8 * b : 8 * b + 8, :], 0, 1)
    for i in range(reach):
        ext[i] = pltpu.roll(ext[i + half_x], rows, axis=0)
        ext[reach + half_x + i] = pltpu.roll(ext[reach + i], rows, axis=0)

    def chunk_of(step):
        return lax.rem(me + 1 + step, half)

    def exchange(q):
        return pltpu.make_async_remote_copy(
            src_ref=zbuf.at[q, core],
            dst_ref=zbuf.at[q, core],
            send_sem=zsend_sem.at[q],
            recv_sem=zrecv_sem.at[q],
            device_id={"comp": 1 - core},
            device_id_type=MESH,
        )

    def deliver(q, h):
        p = h * half + q
        return pltpu.make_async_remote_copy(
            src_ref=msend.at[q, h],
            dst_ref=mrecv.at[me],
            send_sem=msend_sem.at[p],
            recv_sem=mrecv_sem.at[me],
            device_id={"tile": p},
            device_id_type=MESH,
        )

    def zonal(q):
        base = pl.multiple_of(q * width, width)
        total = jnp.zeros((width, 8, lanes), F32)
        for k in range(taps):
            total = total + kx[k : k + 1, :][None] * ext[pl.ds(base + k, width)]
        cells = jnp.swapaxes(total, 0, 1) * mask[:, pl.ds(base, width), :]
        zbuf[q, core] = cells.astype(BF16)

    def finish(q):
        exchange(q).wait_recv()
        lhs = jnp.concatenate(
            [zbuf[q, c].reshape(8 * width, lanes) for c in range(2)], axis=-1
        )
        mixed = lax.dot_general(
            lhs, bal[0], (((1,), (1,)), ((), ())), preferred_element_type=F32
        )
        msend[q] = mixed.astype(BF16).reshape(2, rows, width, lanes)
        for h in range(2):
            p = h * half + q

            @pl.when(p == me)
            def _():
                mrecv[me] = msend[q, h]

            @pl.when(p != me)
            def _():
                deliver(q, h).start()

    loads[2].wait()
    zonal(chunk_of(0))
    pl.semaphore_wait(barrier, tiles)
    exchange(chunk_of(0)).start()
    loads[3].wait()

    lag = min(2, half - 1)
    for step in range(1, lag):
        zonal(chunk_of(step))
        exchange(chunk_of(step)).start()

    @pl.loop(lag, half)
    def _(step):
        zonal(chunk_of(step))
        exchange(chunk_of(step)).start()
        finish(chunk_of(step - lag))

    @pl.loop(half - lag, half)
    def _(step):
        finish(chunk_of(step))

    loads[4].wait()
    acc[...] = jnp.zeros_like(acc)
    window = min(tiles, 2 * -(-reach_y // rows) + 1)
    near = window // 2 if window < tiles else 0
    margin = (taps_y.shape[0] - taps) // 2
    taps_y[...] = jnp.zeros_like(taps_y)
    for k in range(taps):
        taps_y[margin + k] = jnp.broadcast_to(ky[k : k + 1, :], (8, lanes))

    def gather(s):
        @pl.when(s != me)
        def _():
            pltpu.make_async_remote_copy(
                src_ref=mrecv.at[s],
                dst_ref=mrecv.at[s],
                send_sem=msend_sem.at[s],
                recv_sem=mrecv_sem.at[s],
                device_id={"tile": s},
                device_id_type=MESH,
            ).wait_recv()

        band = mrecv[s].astype(F32).reshape(rows, width // 8, 8, lanes)
        first = jnp.minimum(jnp.maximum(s - near, 0), tiles - window)
        for d in range(window):
            b = first + d
            start = rows * (s - b) + reach_y + margin
            for o in range(rows):
                y = rows * b + o
                total = acc[y]
                for i in range(rows):
                    total = total + taps_y[start + i - o][None] * band[i]
                acc[y] = total

    @pl.loop(0, half)
    def _(step):
        s = lax.rem(me + half - 1 - step + tiles, half)
        for h in range(2):
            gather(h * half + s)

    @pl.loop(0, tiles)
    def _(b):
        part = acc[pl.ds(rows * b, rows)]
        out_ref[pl.ds(rows * b, rows)] = part.reshape(rows, width, lanes).astype(BF16)

    @pl.loop(0, half)
    def _(q):
        exchange(q).wait_send()
        for h in range(2):
            @pl.when(h * half + q != me)
            def _():
                deliver(q, h).wait_send()


def per_device(tiles, increment, land_sea, kernel_x, kernel_y, balance):
    rows, columns, lanes = increment.shape
    taps = kernel_x.shape[0]
    reach = (taps - 1) // 2
    half_x, half, width = columns // 2, tiles // 2, columns // tiles
    ny = rows * tiles
    window = min(tiles, 2 * -(-reach // rows) + 1)
    margin = max(rows * (window - 1) + rows - 1 - reach, 0)
    vmem = pltpu.VMEM
    return pl.pallas_call(
        functools.partial(kernel, tiles, reach),
        out_shape=jax.ShapeDtypeStruct((ny, width, lanes), BF16),
        in_specs=[pl.BlockSpec(memory_space=pltpu.HBM)] * 5,
        out_specs=pl.BlockSpec(memory_space=pltpu.VMEM),
        scratch_shapes=[
            vmem(increment.shape, BF16),
            vmem(land_sea.shape, jnp.int32),
            vmem(kernel_x.shape, F32),
            vmem(kernel_y.shape, F32),
            vmem(balance.shape, BF16),
            vmem((8, columns), F32),
            vmem((2 * rows, half_x, lanes), F32),
            vmem((2 * rows, half_x, lanes), F32),
            vmem((half_x + 2 * reach, 8, lanes), F32),
            vmem((half, 2, 2 * rows, width, lanes), BF16),
            vmem((half, 2, rows, width, lanes), BF16),
            vmem((tiles, rows, width, lanes), BF16),
            vmem((taps + 2 * margin, 8, lanes), F32),
            vmem((ny, width // 8, 8, lanes), F32),
            pltpu.SemaphoreType.DMA((5,)),
            pltpu.SemaphoreType.DMA((half,)),
            pltpu.SemaphoreType.DMA((half,)),
            pltpu.SemaphoreType.DMA((tiles,)),
            pltpu.SemaphoreType.DMA((tiles,)),
        ],
        compiler_params=pltpu.CompilerParams(
            collective_id=0, has_side_effects=True, vmem_limit_bytes=63 * 1024 * 1024
        ),
    )(increment, land_sea, kernel_x, kernel_y, balance)


def solution(mesh):
    return jax.shard_map(
        functools.partial(per_device, mesh.shape["tile"]),
        mesh=mesh,
        in_specs=(
            P(("ens", "tile"), None, "comp"),
            P("tile", None),
            P(None, "comp"),
            P(None, "comp"),
            P("tile", "comp", None),
        ),
        out_specs=P("ens", "tile", "comp"),
        check_vma=False,
    )
```

```python
import functools

import jax
import jax.numpy as jnp
from jax import lax
from jax.experimental import pallas as pl
from jax.experimental.pallas import tpu as pltpu
from jax.sharding import PartitionSpec as P

MESH = pl.DeviceIdType.MESH
F32 = jnp.float32
BF16 = jnp.bfloat16


def kernel(
    tiles, reach,
    inc_hbm, sea_hbm, kx_hbm, ky_hbm, bal_hbm, out_ref,
    inc, sea, kx, ky, bal, sea8, mask, nat, ext, zbuf, msend, mrecv, taps_y, acc,
    in_sem, zsend_sem, zrecv_sem, msend_sem, mrecv_sem,
):
    me = lax.axis_index("tile")
    core = lax.axis_index("comp")
    rows, columns, lanes = inc.shape
    half_x = columns // 2
    half = tiles // 2
    width = columns // tiles
    taps = kx.shape[0]
    reach_y = (taps - 1) // 2

    loads = [
        pltpu.make_async_copy(src, dst, in_sem.at[n])
        for n, (src, dst) in enumerate(
            ((sea_hbm, sea), (inc_hbm, inc), (kx_hbm, kx), (bal_hbm, bal), (ky_hbm, ky))
        )
    ]
    for load in loads:
        load.start()

    barrier = pltpu.get_barrier_semaphore()

    @pl.loop(1, tiles)
    def _(d):
        pl.semaphore_signal(
            barrier, inc=1, device_id={"tile": lax.rem(me + d, tiles)}, device_id_type=MESH
        )

    pl.semaphore_signal(barrier, inc=1, device_id={"comp": 1 - core}, device_id_type=MESH)

    loads[0].wait()
    sea8[...] = jnp.zeros_like(sea8)
    sea8[0:rows] = sea[...].astype(F32)
    row_of = lax.broadcasted_iota(jnp.int32, (8, lanes), 0)
    for r in range(rows):
        spread = lax.dot_general(
            sea8[...], (row_of == r).astype(F32), (((0,), (0,)), ((), ())),
            preferred_element_type=F32,
        )
        for h in range(2):
            mask[h * rows + r] = spread[h * half_x : (h + 1) * half_x]

    loads[1].wait()
    for r in range(rows):
        for h in range(2):
            j = h * rows + r
            nat[j] = inc[r, h * half_x : (h + 1) * half_x, :].astype(F32) * mask[j]
    for b in range(half_x // 8):
        ext[reach + 8 * b : reach + 8 * b + 8] = jnp.swapaxes(nat[:, 8 * b : 8 * b + 8, :], 0, 1)
    for i in range(reach):
        ext[i] = pltpu.roll(ext[i + half_x], rows, axis=0)
        ext[reach + half_x + i] = pltpu.roll(ext[reach + i], rows, axis=0)

    def chunk_of(step):
        return lax.rem(me + 1 + step, half)

    def exchange(q):
        return pltpu.make_async_remote_copy(
            src_ref=zbuf.at[q, core],
            dst_ref=zbuf.at[q, core],
            send_sem=zsend_sem.at[q],
            recv_sem=zrecv_sem.at[q],
            device_id={"comp": 1 - core},
            device_id_type=MESH,
        )

    def deliver(q, h):
        p = h * half + q
        return pltpu.make_async_remote_copy(
            src_ref=msend.at[q, h],
            dst_ref=mrecv.at[me],
            send_sem=msend_sem.at[p],
            recv_sem=mrecv_sem.at[me],
            device_id={"tile": p},
            device_id_type=MESH,
        )

    def zonal(q):
        base = pl.multiple_of(q * width, width)
        total = jnp.zeros((width, 8, lanes), F32)
        for k in range(taps):
            total = total + kx[k : k + 1, :][None] * ext[pl.ds(base + k, width)]
        cells = jnp.swapaxes(total, 0, 1) * mask[:, pl.ds(base, width), :]
        zbuf[q, core] = cells.astype(BF16)

    def finish(q):
        exchange(q).wait_recv()
        lhs = jnp.concatenate(
            [zbuf[q, c].reshape(8 * width, lanes) for c in range(2)], axis=-1
        )
        mixed = lax.dot_general(
            lhs, bal[0], (((1,), (1,)), ((), ())), preferred_element_type=F32
        )
        msend[q] = mixed.astype(BF16).reshape(2, rows, width, lanes)
        for h in range(2):
            p = h * half + q

            @pl.when(p == me)
            def _():
                mrecv[me] = msend[q, h]

            @pl.when(p != me)
            def _():
                deliver(q, h).start()

    loads[2].wait()
    zonal(chunk_of(0))
    pl.semaphore_wait(barrier, tiles)
    exchange(chunk_of(0)).start()
    loads[3].wait()

    lag = min(2, half - 1)
    for step in range(1, lag):
        zonal(chunk_of(step))
        exchange(chunk_of(step)).start()

    @pl.loop(lag, half)
    def _(step):
        zonal(chunk_of(step))
        exchange(chunk_of(step)).start()
        finish(chunk_of(step - lag))

    @pl.loop(half - lag, half)
    def _(step):
        finish(chunk_of(step))

    loads[4].wait()
    acc[...] = jnp.zeros_like(acc)
    window = min(tiles, 2 * -(-reach_y // rows) + 1)
    near = window // 2 if window < tiles else 0
    margin = (taps_y.shape[0] - taps) // 2
    taps_y[...] = jnp.zeros_like(taps_y)
    for k in range(taps):
        taps_y[margin + k] = jnp.broadcast_to(ky[k : k + 1, :], (8, lanes))

    def gather(s):
        @pl.when(s != me)
        def _():
            pltpu.make_async_remote_copy(
                src_ref=mrecv.at[s],
                dst_ref=mrecv.at[s],
                send_sem=msend_sem.at[s],
                recv_sem=mrecv_sem.at[s],
                device_id={"tile": s},
                device_id_type=MESH,
            ).wait_recv()

        band = mrecv[s].astype(F32).reshape(rows, width // 8, 8, lanes)
        first = jnp.minimum(jnp.maximum(s - near, 0), tiles - window)
        for d in range(window):
            b = first + d
            start = rows * (s - b) + reach_y + margin
            for o in range(rows):
                y = rows * b + o
                total = acc[y]
                for i in range(rows):
                    total = total + taps_y[start + i - o][None] * band[i]
                acc[y] = total

    @pl.loop(0, half)
    def _(step):
        s = lax.rem(me + half - 1 - step + tiles, half)
        for h in range(2):
            gather(h * half + s)

    @pl.loop(0, tiles)
    def _(b):
        part = acc[pl.ds(rows * b, rows)]
        out_ref[pl.ds(rows * b, rows)] = part.reshape(rows, width, lanes).astype(BF16)

    @pl.loop(0, half)
    def _(q):
        exchange(q).wait_send()
        for h in range(2):
            @pl.when(h * half + q != me)
            def _():
                deliver(q, h).wait_send()


def per_device(tiles, increment, land_sea, kernel_x, kernel_y, balance):
    rows, columns, lanes = increment.shape
    taps = kernel_x.shape[0]
    reach = (taps - 1) // 2
    half_x, half, width = columns // 2, tiles // 2, columns // tiles
    ny = rows * tiles
    window = min(tiles, 2 * -(-reach // rows) + 1)
    margin = max(rows * (window - 1) + rows - 1 - reach, 0)
    vmem = pltpu.VMEM
    return pl.pallas_call(
        functools.partial(kernel, tiles, reach),
        out_shape=jax.ShapeDtypeStruct((ny, width, lanes), BF16),
        in_specs=[pl.BlockSpec(memory_space=pltpu.HBM)] * 5,
        out_specs=pl.BlockSpec(memory_space=pltpu.VMEM),
        scratch_shapes=[
            vmem(increment.shape, BF16),
            vmem(land_sea.shape, jnp.int32),
            vmem(kernel_x.shape, F32),
            vmem(kernel_y.shape, F32),
            vmem(balance.shape, BF16),
            vmem((8, columns), F32),
            vmem((2 * rows, half_x, lanes), F32),
            vmem((2 * rows, half_x, lanes), F32),
            vmem((half_x + 2 * reach, 8, lanes), F32),
            vmem((half, 2, 2 * rows, width, lanes), BF16),
            vmem((half, 2, rows, width, lanes), BF16),
            vmem((tiles, rows, width, lanes), BF16),
            vmem((taps + 2 * margin, 8, lanes), F32),
            vmem((ny, width // 8, 8, lanes), F32),
            pltpu.SemaphoreType.DMA((5,)),
            pltpu.SemaphoreType.DMA((half,)),
            pltpu.SemaphoreType.DMA((half,)),
            pltpu.SemaphoreType.DMA((tiles,)),
            pltpu.SemaphoreType.DMA((tiles,)),
        ],
        compiler_params=pltpu.CompilerParams(
            collective_id=0, has_side_effects=True, vmem_limit_bytes=48 * 1024 * 1024
        ),
    )(*(pltpu.with_memory_space_constraint(a, pltpu.HBM) for a in (increment, land_sea, kernel_x, kernel_y, balance)))


def solution(mesh):
    return jax.shard_map(
        functools.partial(per_device, mesh.shape["tile"]),
        mesh=mesh,
        in_specs=(
            P(("ens", "tile"), None, "comp"),
            P("tile", None),
            P(None, "comp"),
            P(None, "comp"),
            P("tile", "comp", None),
        ),
        out_specs=P("ens", "tile", "comp"),
        check_vma=False,
    )
```

```python
import functools

import jax
import jax.numpy as jnp
from jax import lax
from jax.experimental import pallas as pl
from jax.experimental.pallas import tpu as pltpu
from jax.sharding import PartitionSpec as P

MESH = pl.DeviceIdType.MESH
F32 = jnp.float32
BF16 = jnp.bfloat16


def kernel(
    tiles, reach,
    inc_hbm, sea_hbm, kx_hbm, ky_hbm, bal_hbm, out_ref,
    inc, sea, kx, ky, bal, sea8, mask, nat, ext, zbuf, msend, mrecv, taps_y, acc,
    in_sem, zsend_sem, zrecv_sem, msend_sem, mrecv_sem,
):
    me = lax.axis_index("tile")
    core = lax.axis_index("comp")
    rows, columns, lanes = inc.shape
    half_x = columns // 2
    half = tiles // 2
    width = columns // tiles
    taps = kx.shape[0]
    reach_y = (taps - 1) // 2

    loads = [
        pltpu.make_async_copy(src, dst, in_sem.at[n])
        for n, (src, dst) in enumerate(
            ((sea_hbm, sea), (inc_hbm, inc), (kx_hbm, kx), (bal_hbm, bal), (ky_hbm, ky))
        )
    ]
    barrier = pltpu.get_barrier_semaphore()

    @pl.loop(1, tiles)
    def _(d):
        pl.semaphore_signal(
            barrier, inc=1, device_id={"tile": lax.rem(me + d, tiles)}, device_id_type=MESH
        )

    pl.semaphore_signal(barrier, inc=1, device_id={"comp": 1 - core}, device_id_type=MESH)

    for load in loads:
        load.start()

    loads[0].wait()
    sea8[...] = jnp.zeros_like(sea8)
    sea8[0:rows] = sea[...].astype(F32)
    row_of = lax.broadcasted_iota(jnp.int32, (8, lanes), 0)
    for r in range(rows):
        spread = lax.dot_general(
            sea8[...], (row_of == r).astype(F32), (((0,), (0,)), ((), ())),
            preferred_element_type=F32,
        )
        for h in range(2):
            mask[h * rows + r] = spread[h * half_x : (h + 1) * half_x]

    loads[1].wait()
    for r in range(rows):
        for h in range(2):
            j = h * rows + r
            nat[j] = inc[r, h * half_x : (h + 1) * half_x, :].astype(F32) * mask[j]
    for b in range(half_x // 8):
        ext[reach + 8 * b : reach + 8 * b + 8] = jnp.swapaxes(nat[:, 8 * b : 8 * b + 8, :], 0, 1)
    for i in range(reach):
        ext[i] = pltpu.roll(ext[i + half_x], rows, axis=0)
        ext[reach + half_x + i] = pltpu.roll(ext[reach + i], rows, axis=0)

    def chunk_of(step):
        return lax.rem(me + 1 + step, half)

    def exchange(q):
        return pltpu.make_async_remote_copy(
            src_ref=zbuf.at[q, core],
            dst_ref=zbuf.at[q, core],
            send_sem=zsend_sem.at[q],
            recv_sem=zrecv_sem.at[q],
            device_id={"comp": 1 - core},
            device_id_type=MESH,
        )

    def deliver(q, h):
        p = h * half + q
        return pltpu.make_async_remote_copy(
            src_ref=msend.at[q, h],
            dst_ref=mrecv.at[me],
            send_sem=msend_sem.at[p],
            recv_sem=mrecv_sem.at[me],
            device_id={"tile": p},
            device_id_type=MESH,
        )

    def zonal(q):
        base = pl.multiple_of(q * width, width)
        parts = []
        for g in range(0, width, 8):
            seen = ext[pl.ds(base + g, 8 + taps - 1)]
            total = jnp.zeros((8, 8, lanes), F32)
            for k in range(taps):
                total = total + kx[k : k + 1, :][None] * seen[k : k + 8]
            cells = jnp.swapaxes(total, 0, 1)
            parts.append(cells * mask[:, pl.ds(base + g, 8), :])
        cells = jnp.concatenate(parts, axis=1)
        zbuf[q, core] = cells.astype(BF16)

    def finish(q):
        exchange(q).wait_recv()
        lhs = jnp.concatenate(
            [zbuf[q, c].reshape(8 * width, lanes) for c in range(2)], axis=-1
        )
        mixed = lax.dot_general(
            lhs, bal[0], (((1,), (1,)), ((), ())), preferred_element_type=F32
        )
        msend[q] = mixed.astype(BF16).reshape(2, rows, width, lanes)
        for h in range(2):
            p = h * half + q

            @pl.when(p == me)
            def _():
                mrecv[me] = msend[q, h]

            @pl.when(p != me)
            def _():
                deliver(q, h).start()

    loads[2].wait()
    zonal(chunk_of(0))
    pl.semaphore_wait(barrier, tiles)
    exchange(chunk_of(0)).start()
    loads[3].wait()

    lag = min(2, half - 1)
    for step in range(1, lag):
        zonal(chunk_of(step))
        exchange(chunk_of(step)).start()

    @pl.loop(lag, half)
    def _(step):
        zonal(chunk_of(step))
        exchange(chunk_of(step)).start()
        finish(chunk_of(step - lag))

    @pl.loop(half - lag, half)
    def _(step):
        finish(chunk_of(step))

    loads[4].wait()
    acc[...] = jnp.zeros_like(acc)
    window = min(tiles, 2 * -(-reach_y // rows) + 1)
    near = window // 2 if window < tiles else 0
    margin = (taps_y.shape[0] - taps) // 2
    taps_y[...] = jnp.zeros_like(taps_y)
    for k in range(taps):
        taps_y[margin + k] = jnp.broadcast_to(ky[k : k + 1, :], (8, lanes))

    def gather(s):
        @pl.when(s != me)
        def _():
            pltpu.make_async_remote_copy(
                src_ref=mrecv.at[s],
                dst_ref=mrecv.at[s],
                send_sem=msend_sem.at[s],
                recv_sem=mrecv_sem.at[s],
                device_id={"tile": s},
                device_id_type=MESH,
            ).wait_recv()

        band = mrecv[s].astype(F32).reshape(rows, width // 8, 8, lanes)
        first = jnp.minimum(jnp.maximum(s - near, 0), tiles - window)
        for d in range(window):
            b = first + d
            start = rows * (s - b) + reach_y + margin
            for o in range(rows):
                y = rows * b + o
                total = acc[y]
                for i in range(rows):
                    total = total + taps_y[start + i - o][None] * band[i]
                acc[y] = total

    @pl.loop(0, half)
    def _(step):
        s = lax.rem(me + half - 1 - step + tiles, half)
        for h in range(2):
            gather(h * half + s)

    @pl.loop(0, tiles)
    def _(b):
        part = acc[pl.ds(rows * b, rows)]
        out_ref[pl.ds(rows * b, rows)] = part.reshape(rows, width, lanes).astype(BF16)

    @pl.loop(0, half)
    def _(q):
        exchange(q).wait_send()
        for h in range(2):
            @pl.when(h * half + q != me)
            def _():
                deliver(q, h).wait_send()


def per_device(tiles, increment, land_sea, kernel_x, kernel_y, balance):
    rows, columns, lanes = increment.shape
    taps = kernel_x.shape[0]
    reach = (taps - 1) // 2
    half_x, half, width = columns // 2, tiles // 2, columns // tiles
    ny = rows * tiles
    window = min(tiles, 2 * -(-reach // rows) + 1)
    margin = max(rows * (window - 1) + rows - 1 - reach, 0)
    vmem = pltpu.VMEM
    return pl.pallas_call(
        functools.partial(kernel, tiles, reach),
        out_shape=jax.ShapeDtypeStruct((ny, width, lanes), BF16),
        in_specs=[pl.BlockSpec(memory_space=pltpu.HBM)] * 5,
        out_specs=pl.BlockSpec(memory_space=pltpu.VMEM),
        scratch_shapes=[
            vmem(increment.shape, BF16),
            vmem(land_sea.shape, jnp.int32),
            vmem(kernel_x.shape, F32),
            vmem(kernel_y.shape, F32),
            vmem(balance.shape, BF16),
            vmem((8, columns), F32),
            vmem((2 * rows, half_x, lanes), F32),
            vmem((2 * rows, half_x, lanes), F32),
            vmem((half_x + 2 * reach, 8, lanes), F32),
            vmem((half, 2, 2 * rows, width, lanes), BF16),
            vmem((half, 2, rows, width, lanes), BF16),
            vmem((tiles, rows, width, lanes), BF16),
            vmem((taps + 2 * margin, 8, lanes), F32),
            vmem((ny, width // 8, 8, lanes), F32),
            pltpu.SemaphoreType.DMA((5,)),
            pltpu.SemaphoreType.DMA((half,)),
            pltpu.SemaphoreType.DMA((half,)),
            pltpu.SemaphoreType.DMA((tiles,)),
            pltpu.SemaphoreType.DMA((tiles,)),
        ],
        compiler_params=pltpu.CompilerParams(
            collective_id=0, has_side_effects=True, vmem_limit_bytes=48 * 1024 * 1024
        ),
    )(*(pltpu.with_memory_space_constraint(a, pltpu.HBM) for a in (increment, land_sea, kernel_x, kernel_y, balance)))


def solution(mesh):
    return jax.shard_map(
        functools.partial(per_device, mesh.shape["tile"]),
        mesh=mesh,
        in_specs=(
            P(("ens", "tile"), None, "comp"),
            P("tile", None),
            P(None, "comp"),
            P(None, "comp"),
            P("tile", "comp", None),
        ),
        out_specs=P("ens", "tile", "comp"),
        check_vma=False,
    )
```

```python
import functools

import jax
import jax.numpy as jnp
from jax import lax
from jax.experimental import pallas as pl
from jax.experimental.pallas import tpu as pltpu
from jax.sharding import PartitionSpec as P

MESH = pl.DeviceIdType.MESH
F32 = jnp.float32
BF16 = jnp.bfloat16


def kernel(
    tiles, reach,
    inc_hbm, sea_hbm, kx_hbm, ky_hbm, bal_hbm, out_ref,
    inc, sea, kx, ky, bal, sea8, mask, nat, ext, zbuf, msend, mrecv, taps_y, acc,
    in_sem, zsend_sem, zrecv_sem, msend_sem, mrecv_sem,
):
    me = lax.axis_index("tile")
    core = lax.axis_index("comp")
    rows, columns, lanes = inc.shape
    half_x = columns // 2
    half = tiles // 2
    width = columns // tiles
    taps = kx.shape[0]
    reach_y = (taps - 1) // 2

    loads = [
        pltpu.make_async_copy(src, dst, in_sem.at[n])
        for n, (src, dst) in enumerate(
            ((sea_hbm, sea), (inc_hbm, inc), (kx_hbm, kx), (bal_hbm, bal), (ky_hbm, ky))
        )
    ]
    for load in loads:
        load.start()

    barrier = pltpu.get_barrier_semaphore()

    @pl.loop(1, tiles)
    def _(d):
        pl.semaphore_signal(
            barrier, inc=1, device_id={"tile": lax.rem(me + d, tiles)}, device_id_type=MESH
        )

    pl.semaphore_signal(barrier, inc=1, device_id={"comp": 1 - core}, device_id_type=MESH)

    loads[0].wait()
    sea8[...] = jnp.zeros_like(sea8)
    sea8[0:rows] = sea[...].astype(F32)
    row_of = lax.broadcasted_iota(jnp.int32, (8, lanes), 0)
    for r in range(rows):
        spread = lax.dot_general(
            sea8[...], (row_of == r).astype(F32), (((0,), (0,)), ((), ())),
            preferred_element_type=F32,
        )
        for h in range(2):
            mask[h * rows + r] = spread[h * half_x : (h + 1) * half_x]

    loads[1].wait()
    for r in range(rows):
        for h in range(2):
            j = h * rows + r
            nat[j] = inc[r, h * half_x : (h + 1) * half_x, :].astype(F32) * mask[j]
    for b in range(half_x // 8):
        ext[reach + 8 * b : reach + 8 * b + 8] = jnp.swapaxes(nat[:, 8 * b : 8 * b + 8, :], 0, 1)
    for i in range(reach):
        ext[i] = pltpu.roll(ext[i + half_x], rows, axis=0)
        ext[reach + half_x + i] = pltpu.roll(ext[reach + i], rows, axis=0)

    def chunk_of(step):
        return lax.rem(me + 1 + step, half)

    def exchange(q):
        return pltpu.make_async_remote_copy(
            src_ref=zbuf.at[q, core],
            dst_ref=zbuf.at[q, core],
            send_sem=zsend_sem.at[q],
            recv_sem=zrecv_sem.at[q],
            device_id={"comp": 1 - core},
            device_id_type=MESH,
        )

    def deliver(q, h):
        p = h * half + q
        return pltpu.make_async_remote_copy(
            src_ref=msend.at[q, h],
            dst_ref=mrecv.at[me],
            send_sem=msend_sem.at[p],
            recv_sem=mrecv_sem.at[me],
            device_id={"tile": p},
            device_id_type=MESH,
        )

    def zonal(q):
        base = pl.multiple_of(q * width, width)
        total = jnp.zeros((width, 8, lanes), F32)
        for k in range(taps):
            total = total + kx[k : k + 1, :][None] * ext[pl.ds(base + k, width)]
        cells = jnp.swapaxes(total, 0, 1) * mask[:, pl.ds(base, width), :]
        zbuf[q, core] = cells.astype(BF16)

    def finish(q):
        exchange(q).wait_recv()
        lhs = jnp.concatenate(
            [zbuf[q, c].reshape(8 * width, lanes) for c in range(2)], axis=-1
        )
        mixed = lax.dot_general(
            lhs, bal[0], (((1,), (1,)), ((), ())), preferred_element_type=F32
        )
        msend[q] = mixed.astype(BF16).reshape(2, rows, width, lanes)
        for h in range(2):
            p = h * half + q

            @pl.when(p == me)
            def _():
                mrecv[me] = msend[q, h]

            @pl.when(p != me)
            def _():
                deliver(q, h).start()

    loads[2].wait()
    zonal(chunk_of(0))
    pl.semaphore_wait(barrier, tiles)
    exchange(chunk_of(0)).start()
    loads[3].wait()

    lag = min(1, half - 1)
    for step in range(1, lag):
        zonal(chunk_of(step))
        exchange(chunk_of(step)).start()

    @pl.loop(lag, half)
    def _(step):
        zonal(chunk_of(step))
        exchange(chunk_of(step)).start()
        finish(chunk_of(step - lag))

    @pl.loop(half - lag, half)
    def _(step):
        finish(chunk_of(step))

    loads[4].wait()
    acc[...] = jnp.zeros_like(acc)
    window = min(tiles, 2 * -(-reach_y // rows) + 1)
    near = window // 2 if window < tiles else 0
    margin = (taps_y.shape[0] - taps) // 2
    taps_y[...] = jnp.zeros_like(taps_y)
    for k in range(taps):
        taps_y[margin + k] = jnp.broadcast_to(ky[k : k + 1, :], (8, lanes))

    def gather(s):
        @pl.when(s != me)
        def _():
            pltpu.make_async_remote_copy(
                src_ref=mrecv.at[s],
                dst_ref=mrecv.at[s],
                send_sem=msend_sem.at[s],
                recv_sem=mrecv_sem.at[s],
                device_id={"tile": s},
                device_id_type=MESH,
            ).wait_recv()

        band = mrecv[s].astype(F32).reshape(rows, width // 8, 8, lanes)
        first = jnp.minimum(jnp.maximum(s - near, 0), tiles - window)
        for d in range(window):
            b = first + d
            start = rows * (s - b) + reach_y + margin
            for o in range(rows):
                y = rows * b + o
                total = acc[y]
                for i in range(rows):
                    total = total + taps_y[start + i - o][None] * band[i]
                acc[y] = total

    @pl.loop(0, half)
    def _(step):
        s = lax.rem(me + half - 1 - step + tiles, half)
        for h in range(2):
            gather(h * half + s)

    @pl.loop(0, tiles)
    def _(b):
        part = acc[pl.ds(rows * b, rows)]
        out_ref[pl.ds(rows * b, rows)] = part.reshape(rows, width, lanes).astype(BF16)

    @pl.loop(0, half)
    def _(q):
        exchange(q).wait_send()
        for h in range(2):
            @pl.when(h * half + q != me)
            def _():
                deliver(q, h).wait_send()


def per_device(tiles, increment, land_sea, kernel_x, kernel_y, balance):
    rows, columns, lanes = increment.shape
    taps = kernel_x.shape[0]
    reach = (taps - 1) // 2
    half_x, half, width = columns // 2, tiles // 2, columns // tiles
    ny = rows * tiles
    window = min(tiles, 2 * -(-reach // rows) + 1)
    margin = max(rows * (window - 1) + rows - 1 - reach, 0)
    vmem = pltpu.VMEM
    return pl.pallas_call(
        functools.partial(kernel, tiles, reach),
        out_shape=jax.ShapeDtypeStruct((ny, width, lanes), BF16),
        in_specs=[pl.BlockSpec(memory_space=pltpu.HBM)] * 5,
        out_specs=pl.BlockSpec(memory_space=pltpu.VMEM),
        scratch_shapes=[
            vmem(increment.shape, BF16),
            vmem(land_sea.shape, jnp.int32),
            vmem(kernel_x.shape, F32),
            vmem(kernel_y.shape, F32),
            vmem(balance.shape, BF16),
            vmem((8, columns), F32),
            vmem((2 * rows, half_x, lanes), F32),
            vmem((2 * rows, half_x, lanes), F32),
            vmem((half_x + 2 * reach, 8, lanes), F32),
            vmem((half, 2, 2 * rows, width, lanes), BF16),
            vmem((half, 2, rows, width, lanes), BF16),
            vmem((tiles, rows, width, lanes), BF16),
            vmem((taps + 2 * margin, 8, lanes), F32),
            vmem((ny, width // 8, 8, lanes), F32),
            pltpu.SemaphoreType.DMA((5,)),
            pltpu.SemaphoreType.DMA((half,)),
            pltpu.SemaphoreType.DMA((half,)),
            pltpu.SemaphoreType.DMA((tiles,)),
            pltpu.SemaphoreType.DMA((tiles,)),
        ],
        compiler_params=pltpu.CompilerParams(
            collective_id=0, has_side_effects=True, vmem_limit_bytes=48 * 1024 * 1024
        ),
    )(*(pltpu.with_memory_space_constraint(a, pltpu.HBM) for a in (increment, land_sea, kernel_x, kernel_y, balance)))


def solution(mesh):
    return jax.shard_map(
        functools.partial(per_device, mesh.shape["tile"]),
        mesh=mesh,
        in_specs=(
            P(("ens", "tile"), None, "comp"),
            P("tile", None),
            P(None, "comp"),
            P(None, "comp"),
            P("tile", "comp", None),
        ),
        out_specs=P("ens", "tile", "comp"),
        check_vma=False,
    )
```

```python
import functools

import jax
import jax.numpy as jnp
from jax import lax
from jax.experimental import pallas as pl
from jax.experimental.pallas import tpu as pltpu
from jax.sharding import PartitionSpec as P

MESH = pl.DeviceIdType.MESH
F32 = jnp.float32
BF16 = jnp.bfloat16


def kernel(
    tiles, reach,
    inc_hbm, sea_hbm, kx_hbm, ky_hbm, bal_hbm, out_ref,
    inc, sea, kx, ky, bal, sea8, mask, nat, ext, zbuf, msend, mrecv, taps_y, acc,
    in_sem, zsend_sem, zrecv_sem, msend_sem, mrecv_sem,
):
    me = lax.axis_index("tile")
    core = lax.axis_index("comp")
    rows, columns, lanes = inc.shape
    half_x = columns // 2
    half = tiles // 2
    width = columns // tiles
    taps = kx.shape[0]
    reach_y = (taps - 1) // 2

    loads = [
        pltpu.make_async_copy(src, dst, in_sem.at[n])
        for n, (src, dst) in enumerate(
            ((sea_hbm, sea), (inc_hbm, inc), (kx_hbm, kx), (bal_hbm, bal), (ky_hbm, ky))
        )
    ]
    for load in loads:
        load.start()

    barrier = pltpu.get_barrier_semaphore()

    @pl.loop(1, tiles)
    def _(d):
        pl.semaphore_signal(
            barrier, inc=1, device_id={"tile": lax.rem(me + d, tiles)}, device_id_type=MESH
        )

    pl.semaphore_signal(barrier, inc=1, device_id={"comp": 1 - core}, device_id_type=MESH)

    loads[0].wait()
    sea8[...] = jnp.zeros_like(sea8)
    sea8[0:rows] = sea[...].astype(F32)
    row_of = lax.broadcasted_iota(jnp.int32, (8, lanes), 0)
    for r in range(rows):
        spread = lax.dot_general(
            sea8[...].astype(BF16), (row_of == r).astype(F32).astype(BF16), (((0,), (0,)), ((), ())),
            preferred_element_type=F32,
        )
        for h in range(2):
            mask[h * rows + r] = spread[h * half_x : (h + 1) * half_x]

    loads[1].wait()
    for r in range(rows):
        for h in range(2):
            j = h * rows + r
            nat[j] = inc[r, h * half_x : (h + 1) * half_x, :].astype(F32) * mask[j]
    for b in range(half_x // 8):
        ext[reach + 8 * b : reach + 8 * b + 8] = jnp.swapaxes(nat[:, 8 * b : 8 * b + 8, :], 0, 1)
    for i in range(reach):
        ext[i] = pltpu.roll(ext[i + half_x], rows, axis=0)
        ext[reach + half_x + i] = pltpu.roll(ext[reach + i], rows, axis=0)

    def chunk_of(step):
        return lax.rem(me + 1 + step, half)

    def exchange(q):
        return pltpu.make_async_remote_copy(
            src_ref=zbuf.at[q, core],
            dst_ref=zbuf.at[q, core],
            send_sem=zsend_sem.at[q],
            recv_sem=zrecv_sem.at[q],
            device_id={"comp": 1 - core},
            device_id_type=MESH,
        )

    def deliver(q, h):
        p = h * half + q
        return pltpu.make_async_remote_copy(
            src_ref=msend.at[q, h],
            dst_ref=mrecv.at[me],
            send_sem=msend_sem.at[p],
            recv_sem=mrecv_sem.at[me],
            device_id={"tile": p},
            device_id_type=MESH,
        )

    def zonal(q):
        base = pl.multiple_of(q * width, width)
        total = jnp.zeros((width, 8, lanes), F32)
        for k in range(taps):
            total = total + kx[k : k + 1, :][None] * ext[pl.ds(base + k, width)]
        cells = jnp.swapaxes(total, 0, 1) * mask[:, pl.ds(base, width), :]
        zbuf[q, core] = cells.astype(BF16)

    def finish(q):
        exchange(q).wait_recv()
        lhs = jnp.concatenate(
            [zbuf[q, c].reshape(8 * width, lanes) for c in range(2)], axis=-1
        )
        mixed = lax.dot_general(
            lhs, bal[0], (((1,), (1,)), ((), ())), preferred_element_type=F32
        )
        msend[q] = mixed.astype(BF16).reshape(2, rows, width, lanes)
        for h in range(2):
            p = h * half + q

            @pl.when(p == me)
            def _():
                mrecv[me] = msend[q, h]

            @pl.when(p != me)
            def _():
                deliver(q, h).start()

    loads[2].wait()
    zonal(chunk_of(0))
    pl.semaphore_wait(barrier, tiles)
    exchange(chunk_of(0)).start()
    loads[3].wait()

    lag = min(2, half - 1)
    for step in range(1, lag):
        zonal(chunk_of(step))
        exchange(chunk_of(step)).start()

    @pl.loop(lag, half)
    def _(step):
        zonal(chunk_of(step))
        exchange(chunk_of(step)).start()
        finish(chunk_of(step - lag))

    @pl.loop(half - lag, half)
    def _(step):
        finish(chunk_of(step))

    loads[4].wait()
    acc[...] = jnp.zeros_like(acc)
    window = min(tiles, 2 * -(-reach_y // rows) + 1)
    near = window // 2 if window < tiles else 0
    margin = (taps_y.shape[0] - taps) // 2
    taps_y[...] = jnp.zeros_like(taps_y)
    for k in range(taps):
        taps_y[margin + k] = jnp.broadcast_to(ky[k : k + 1, :], (8, lanes))

    def gather(s):
        @pl.when(s != me)
        def _():
            pltpu.make_async_remote_copy(
                src_ref=mrecv.at[s],
                dst_ref=mrecv.at[s],
                send_sem=msend_sem.at[s],
                recv_sem=mrecv_sem.at[s],
                device_id={"tile": s},
                device_id_type=MESH,
            ).wait_recv()

        band = mrecv[s].astype(F32).reshape(rows, width // 8, 8, lanes)
        first = jnp.minimum(jnp.maximum(s - near, 0), tiles - window)
        for d in range(window):
            b = first + d
            start = rows * (s - b) + reach_y + margin
            for o in range(rows):
                y = rows * b + o
                total = acc[y]
                for i in range(rows):
                    total = total + taps_y[start + i - o][None] * band[i]
                acc[y] = total

    @pl.loop(0, half)
    def _(step):
        s = lax.rem(me + half - 1 - step + tiles, half)
        for h in range(2):
            gather(h * half + s)

    @pl.loop(0, tiles)
    def _(b):
        part = acc[pl.ds(rows * b, rows)]
        out_ref[pl.ds(rows * b, rows)] = part.reshape(rows, width, lanes).astype(BF16)

    @pl.loop(0, half)
    def _(q):
        exchange(q).wait_send()
        for h in range(2):
            @pl.when(h * half + q != me)
            def _():
                deliver(q, h).wait_send()


def per_device(tiles, increment, land_sea, kernel_x, kernel_y, balance):
    rows, columns, lanes = increment.shape
    taps = kernel_x.shape[0]
    reach = (taps - 1) // 2
    half_x, half, width = columns // 2, tiles // 2, columns // tiles
    ny = rows * tiles
    window = min(tiles, 2 * -(-reach // rows) + 1)
    margin = max(rows * (window - 1) + rows - 1 - reach, 0)
    vmem = pltpu.VMEM
    return pl.pallas_call(
        functools.partial(kernel, tiles, reach),
        out_shape=jax.ShapeDtypeStruct((ny, width, lanes), BF16),
        in_specs=[pl.BlockSpec(memory_space=pltpu.HBM)] * 5,
        out_specs=pl.BlockSpec(memory_space=pltpu.VMEM),
        scratch_shapes=[
            vmem(increment.shape, BF16),
            vmem(land_sea.shape, jnp.int32),
            vmem(kernel_x.shape, F32),
            vmem(kernel_y.shape, F32),
            vmem(balance.shape, BF16),
            vmem((8, columns), F32),
            vmem((2 * rows, half_x, lanes), F32),
            vmem((2 * rows, half_x, lanes), F32),
            vmem((half_x + 2 * reach, 8, lanes), F32),
            vmem((half, 2, 2 * rows, width, lanes), BF16),
            vmem((half, 2, rows, width, lanes), BF16),
            vmem((tiles, rows, width, lanes), BF16),
            vmem((taps + 2 * margin, 8, lanes), F32),
            vmem((ny, width // 8, 8, lanes), F32),
            pltpu.SemaphoreType.DMA((5,)),
            pltpu.SemaphoreType.DMA((half,)),
            pltpu.SemaphoreType.DMA((half,)),
            pltpu.SemaphoreType.DMA((tiles,)),
            pltpu.SemaphoreType.DMA((tiles,)),
        ],
        compiler_params=pltpu.CompilerParams(
            collective_id=0, has_side_effects=True, vmem_limit_bytes=48 * 1024 * 1024
        ),
    )(*(pltpu.with_memory_space_constraint(a, pltpu.HBM) for a in (increment, land_sea, kernel_x, kernel_y, balance)))


def solution(mesh):
    return jax.shard_map(
        functools.partial(per_device, mesh.shape["tile"]),
        mesh=mesh,
        in_specs=(
            P(("ens", "tile"), None, "comp"),
            P("tile", None),
            P(None, "comp"),
            P(None, "comp"),
            P("tile", "comp", None),
        ),
        out_specs=P("ens", "tile", "comp"),
        check_vma=False,
    )
```
